128 devices in a mesh: tm: 4 (over y_hi, core), head: 32 (over x, y_lo, z).
Axes of the slice: x: 4, y: 4 (y_hi: 2, y_lo: 2; y = y_hi * 2 + y_lo), z: 4, core: 2. Of those that a mesh axis runs over, the one named last changes fastest.
Arguments:
- query: bfloat16 [8, 2048, 4096], P('tm', 'head'), may hold values from -5 to 5
- key_in: bfloat16 [8, 2048, 4096], P('tm', 'head'), may hold values from -5 to 5
- value: bfloat16 [8, 2048, 4096], P('tm', 'head'), may hold values from -6 to 6
- query_dot: bfloat16 [8, 2048, 4096], P('tm', 'head'), may hold values from -6 to 6
- key_dot: bfloat16 [8, 2048, 4096], P('tm', 'head'), may hold values from -6 to 6
- value_dot: bfloat16 [8, 2048, 4096], P('tm', 'head'), may hold values from -6 to 6
Outputs:
- attended: bfloat16 [8, 2048, 4096], P('tm', 'head')
- attended_dot: bfloat16 [8, 2048, 4096], P('tm', 'head')
The draws below stay inside these ranges and needn't reach their ends.
All inputs are finite; a program needn't handle non-finite values.
Results may differ from the reference program's by a relative error of at most 0.0049.
Values may be sent and summed in bfloat16 or wider, within the bound.
A program may use at most 128 MiB of HBM per device.

```python
import math
import jax
import jax.numpy as jnp
from jax import lax

HD = 128
D = 4096
FT = 2048
FRAMES = 8


def draw_query(key, part):
    key = jax.random.fold_in(key, 11)
    rows = FRAMES * FT
    base = jax.random.truncated_normal(key, -4.0, 4.0, (rows, D), jnp.float32)
    return base.reshape(FRAMES, FT, D).astype(jnp.bfloat16)


def draw_key_in(key, part):
    key = jax.random.fold_in(key, 23)
    rows = FRAMES * FT
    base = jax.random.truncated_normal(key, -4.0, 4.0, (rows, D), jnp.float32)
    return base.reshape(FRAMES, FT, D).astype(jnp.bfloat16)


def block_levels(own_key, shape, shards, smallest, largest):
    gain, own = 1.0, jax.random.fold_in(own_key, 6)
    for dim, parts in shards:
        draws = jnp.exp(jax.random.uniform(jax.random.fold_in(own, dim), (parts,), jnp.float32, smallest / len(shards), largest / len(shards)))
        gain = gain * jnp.repeat(draws, shape[dim] // parts).reshape([-1 if axis == dim else 1 for axis in range(len(shape))])
    return gain


def scatter_about(key, dims, scale, reach, pieces=(), held_as=jnp.bfloat16):
    result = jax.random.normal(key, dims, jnp.float32) * scale
    if len(pieces) > 0:
        result = block_levels(key, dims, pieces, -0.22, 0.18) * result
    return jnp.clip(result, min=-reach, max=reach).astype(held_as)


def setup_inputs(seed: int = 0) -> dict:
    key_list = jax.random.split(jax.random.key(seed), 7)
    query = draw_query(jax.random.fold_in(key_list[6], 71), 0)
    key_in = draw_key_in(jax.random.fold_in(key_list[6], 71), 0)
    value = scatter_about(key_list[2], (FRAMES, FT, D), 1.0, 6.0, ((0, 4), (1, 32)))
    query_dot = scatter_about(key_list[3], (FRAMES, FT, D), 1.0, 6.0, ((0, 4), (1, 32)))
    key_dot = scatter_about(key_list[4], (FRAMES, FT, D), 1.0, 6.0, ((0, 4), (1, 32)))
    value_dot = scatter_about(key_list[5], (FRAMES, FT, D), 1.0, 6.0, ((0, 4), (1, 32)))
    return dict(query=query, key_in=key_in, value=value, query_dot=query_dot, key_dot=key_dot, value_dot=value_dot)


def contract(left, right):
    return lax.dot_general(left, right, (((1,), (1,)), ((), ())), preferred_element_type=jnp.float32)

def attend_frame(query_f, query_dot_f, keys, values, keys_dot, values_dot, prior_ok):
    width = query_f.shape[0]
    factor = 1.0 / math.sqrt(query_f.shape[1])
    scores = contract(query_f, keys) * factor
    scores_dot = (contract(query_dot_f, keys) + contract(query_f, keys_dot)) * factor
    valid = (jnp.arange(2 * width) >= width) | prior_ok
    scores = jnp.where(valid[None, :], scores, -1e+30)
    top = lax.optimization_barrier(jnp.max(scores, axis=1, keepdims=True))
    weights = jnp.exp(scores - top)
    probs = weights / lax.optimization_barrier(jnp.sum(weights, axis=1, keepdims=True))
    mean_dot = lax.optimization_barrier(jnp.sum(probs * scores_dot, axis=1, keepdims=True))
    probs_dot = probs * (scores_dot - mean_dot)
    probs_low = probs.astype(jnp.bfloat16)
    probs_dot_low = probs_dot.astype(jnp.bfloat16)
    output = jnp.dot(probs_low, values, preferred_element_type=jnp.float32)
    output_dot = jnp.dot(probs_dot_low, values, preferred_element_type=jnp.float32) + jnp.dot(probs_low, values_dot, preferred_element_type=jnp.float32)
    return (output.astype(jnp.bfloat16), output_dot.astype(jnp.bfloat16))

def reference(query, key_in, value, query_dot, key_dot, value_dot):
    frames, width, model = query.shape
    heads = model // HD

    def split(array):
        return array.reshape(frames, width, heads, HD).transpose(0, 2, 1, 3)
    q_all, qd_all = (split(query), split(query_dot))
    k_all, v_all = (split(key_in), split(value))
    kd_all, vd_all = (split(key_dot), split(value_dot))

    def one_frame(index):
        before = jnp.maximum(index - 1, 0)
        prior_ok = index > 0

        def joined(array):
            return jnp.concatenate([array[before], array[index]], axis=1)
        items = (q_all[index], qd_all[index], joined(k_all), joined(v_all), joined(kd_all), joined(vd_all))
        return lax.map(lambda part: attend_frame(*part, prior_ok), items)
    output, output_dot = lax.map(one_frame, jnp.arange(frames))

    def merge(array):
        return array.transpose(0, 2, 1, 3).reshape(frames, width, model)
    return (merge(output), merge(output_dot))
```

```python
import functools
import math

import jax
import jax.numpy as jnp
from jax import lax
from jax.experimental import pallas as pl
from jax.experimental.pallas import tpu as pltpu
from jax.sharding import PartitionSpec as P

HD = 128
FACTOR = 1.0 / math.sqrt(HD)
LOG2_FACTOR = FACTOR * math.log2(math.e)
MESH = pl.DeviceIdType.MESH
COMPUTE = True
OUTPUTS = True
QS = True
PIECE = 16
ROWS = 256


def contract(left, right):
    return lax.dot_general(
        left, right, (((1,), (1,)), ((), ())), preferred_element_type=jnp.float32
    )


def product(left, right):
    return jnp.dot(left, right, preferred_element_type=jnp.float32)


def frame_part(query, query_dot, key, key_dot, value, value_dot):
    scores = contract(query, key)
    scores_dot = contract(
        jnp.concatenate([query_dot, query], axis=1), jnp.concatenate([key, key_dot], axis=1)
    )
    top = jnp.max(scores, axis=1, keepdims=True)
    weights = jnp.exp2((scores - top) * LOG2_FACTOR)
    total = jnp.sum(weights, axis=1, keepdims=True)
    center = jnp.sum(weights * scores_dot, axis=1, keepdims=True) / total
    weights_dot = (weights * (scores_dot - center)).astype(jnp.bfloat16)
    both = product(weights.astype(jnp.bfloat16), jnp.concatenate([value, value_dot], axis=1))
    return top, total, center, both[:, :HD], both[:, HD:], product(weights_dot, value)


def combine(parts):
    top = functools.reduce(jnp.maximum, [part[0] for part in parts])
    shares = [jnp.exp2((part[0] - top) * LOG2_FACTOR) for part in parts]
    inverse = 1.0 / sum(share * part[1] for share, part in zip(shares, parts))
    shares = [share * inverse for share in shares]
    center = sum(share * part[1] * part[2] for share, part in zip(shares, parts))
    output = sum(share * part[3] for share, part in zip(shares, parts))
    output_dot = sum(
        share * ((part[5] + (part[2] - center) * part[3]) * FACTOR + part[4])
        for share, part in zip(shares, parts)
    )
    return output.astype(jnp.bfloat16), output_dot.astype(jnp.bfloat16)


def kernel(groups, devices, flip, *refs):
    ins, outs, refs = refs[:6], refs[6:8], refs[8:]
    kv_bufs, q_bufs, o_bufs, refs = refs[:4], refs[4:6], refs[6:8], refs[8:]
    kv_send, kv_recv, halo_send, halo_recv, q_send, q_recv, o_send, o_recv = refs
    query, key_in, value, query_dot, key_dot, value_dot = ins
    kvs = (key_in, key_dot, value, value_dot)
    qs = (query, query_dot)
    group, me = lax.axis_index("tm"), lax.axis_index("head")
    tokens = query.shape[1]
    pieces = tokens // PIECE
    first = group == 0
    high = group // 2
    my_head = me ^ (high * flip)
    my_columns = pl.ds(pl.multiple_of(my_head * HD, HD), HD)
    odd = lax.rem(group, 2)
    next_place = (lax.rem(group + 1, groups), me ^ (odd * flip))
    prior_place = (lax.rem(group + groups - 1, groups), me ^ ((1 - odd) * flip))

    barrier = pltpu.get_barrier_semaphore()

    def greet(step, carry):
        peer = lax.rem(me + step, devices)
        pl.semaphore_signal(barrier, inc=1, device_id=(group, peer), device_id_type=MESH)
        return carry

    lax.fori_loop(1, devices, greet, 0)

    for place in (prior_place, next_place):
        pl.semaphore_signal(barrier, inc=1, device_id=place, device_id_type=MESH)
    pl.semaphore_wait(barrier, devices + 1)

    def rows_of(place, size):
        return pl.ds(pl.multiple_of(place * size, size), size)

    def head_columns(peer):
        return pl.ds(pl.multiple_of((peer ^ (high * flip)) * HD, HD), HD)

    def send_keys(frame):
        def one(peer, remote):
            for i, (source, buf) in enumerate(zip(kvs, kv_bufs)):
                src = source.at[frame, :, head_columns(peer)]
                dst = buf.at[frame + 1, rows_of(me, tokens), :]
                if remote:
                    pltpu.make_async_remote_copy(
                        src, dst, kv_send.at[frame, i], kv_recv.at[frame, i],
                        device_id=(group, peer), device_id_type=MESH,
                    ).start()
                else:
                    pltpu.make_async_copy(src, dst, kv_recv.at[frame, i]).start()

        def loop(step, carry):
            one(lax.rem(me + step, devices), True)
            return carry

        lax.fori_loop(1, devices, loop, 0)
        one(me, False)

    def send_queries(frame, piece):
        slot = frame * pieces + piece

        def one(peer, remote):
            for i, (source, buf) in enumerate(zip(qs, q_bufs)):
                src = source.at[frame, pl.ds(piece * PIECE, PIECE), head_columns(peer)]
                dst = buf.at[slot, rows_of(me, PIECE), :]
                if remote:
                    pltpu.make_async_remote_copy(
                        src, dst, q_send.at[slot, i], q_recv.at[slot, i],
                        device_id=(group, peer), device_id_type=MESH,
                    ).start()
                else:
                    pltpu.make_async_copy(src, dst, q_recv.at[slot, i]).start()

        def loop(step, carry):
            one(lax.rem(me + step, devices), True)
            return carry

        lax.fori_loop(1, devices, loop, 0)
        one(me, False)

    def send_outputs(frame, piece):
        slot = frame * pieces + piece

        def one(peer, remote):
            for i, (buf, target) in enumerate(zip(o_bufs, outs)):
                src = buf.at[slot, rows_of(peer, PIECE), :]
                dst = target.at[frame, pl.ds(piece * PIECE, PIECE), my_columns]
                if remote:
                    pltpu.make_async_remote_copy(
                        src, dst, o_send.at[i], o_recv.at[i],
                        device_id=(group, peer), device_id_type=MESH,
                    ).start()
                else:
                    pltpu.make_async_copy(src, dst, o_recv.at[i]).start()

        def loop(step, carry):
            one(lax.rem(me + step, devices), True)
            return carry

        lax.fori_loop(1, devices, loop, 0)
        one(me, False)

    def await_bytes(ref, semaphore):
        pltpu.make_async_copy(ref, ref, semaphore).wait()

    blocks = [(frame, piece) for frame in (1, 0) for piece in range(pieces)]
    send_keys(1)
    send_keys(0)
    if QS:
        for frame, piece in blocks:
            send_queries(frame, piece)

    def halo(buf, i):
        return pltpu.make_async_remote_copy(
            buf.at[2], buf.at[0], halo_send.at[i], halo_recv.at[i],
            device_id=next_place, device_id_type=MESH,
        )

    for i, buf in enumerate(kv_bufs):
        await_bytes(buf.at[2], kv_recv.at[1, i])

    for i, buf in enumerate(kv_bufs):
        halo(buf, i).start()

    for i, buf in enumerate(kv_bufs):
        await_bytes(buf.at[1], kv_recv.at[0, i])

    def block_compute(frame, slot):
        steps = q_bufs[0].shape[1] // ROWS

        def step(index, carry):
            rows = rows_of(index, ROWS)
            q, qd = (buf[slot, rows, :] for buf in q_bufs)
            parts = []
            for key_slot in (frame, frame + 1):
                keys = [buf[key_slot] for buf in kv_bufs]
                parts.append(frame_part(q, qd, *keys))
            if frame == 0:
                top, *rest = parts[0]
                parts[0] = (jnp.where(first, -1e30, top), jnp.where(first, 0.0, rest[0]), *rest[1:])
            output, output_dot = combine(parts)
            o_bufs[0][slot, rows, :] = output
            o_bufs[1][slot, rows, :] = output_dot
            return carry

        lax.fori_loop(0, steps, step, 0)

    for frame in (1, 0):
        if frame == 0:
            for i, buf in enumerate(kv_bufs):
                await_bytes(buf.at[0], halo_recv.at[i])
        for piece in range(pieces):
            slot = frame * pieces + piece
            if QS:
                for i, buf in enumerate(q_bufs):
                    await_bytes(buf.at[slot], q_recv.at[slot, i])
            if COMPUTE:
                block_compute(frame, slot)
            if OUTPUTS:
                send_outputs(frame, piece)

    for i, buf in enumerate(kv_bufs):
        await_bytes(buf.at[2], halo_send.at[i])

    share = (devices - 1) * tokens
    for frame in (0, 1):
        for i, buf in enumerate(kv_bufs):
            await_bytes(buf.at[frame + 1, pl.ds(0, share)], kv_send.at[frame, i])
        for piece in range(pieces):
            if QS:
                for i, buf in enumerate(q_bufs):
                    slot = frame * pieces + piece
                    await_bytes(buf.at[slot, pl.ds(0, (devices - 1) * PIECE)], q_send.at[slot, i])
    if OUTPUTS:
        for i, (buf, target) in enumerate(zip(o_bufs, outs)):
            await_bytes(buf.at[:, pl.ds(0, (devices - 1) * PIECE)], o_send.at[i])
            await_bytes(target, o_recv.at[i])


def per_device(*args):
    groups, devices = lax.axis_size("tm"), lax.axis_size("head")
    frames, tokens, model = args[0].shape
    width = tokens * devices
    slots = frames * tokens // PIECE
    bf16 = jnp.bfloat16
    kv = pltpu.VMEM((frames + 1, width, HD), bf16)
    q = pltpu.VMEM((slots, devices * PIECE, HD), bf16)
    dma = pltpu.SemaphoreType.DMA
    return pl.pallas_call(
        functools.partial(kernel, groups, devices, 4),
        out_shape=[jax.ShapeDtypeStruct((frames, tokens, model), bf16)] * 2,
        in_specs=[pl.BlockSpec(memory_space=pl.ANY)] * 6,
        out_specs=[pl.BlockSpec(memory_space=pl.ANY)] * 2,
        scratch_shapes=[kv] * 4 + [q] * 4
        + [dma((2, 4)), dma((2, 4)), dma((4,)), dma((4,)), dma((slots, 2)), dma((slots, 2)), dma((2,)), dma((2,))],
        compiler_params=pltpu.CompilerParams(
            collective_id=0, has_side_effects=True, vmem_limit_bytes=56 * 1024 * 1024
        ),
    )(*args)


def solution(mesh):
    spec = P("tm", "head", None)
    return jax.shard_map(
        per_device, mesh=mesh, in_specs=(spec,) * 6, out_specs=(spec, spec), check_vma=False
    )
```

```python
import functools
import math

import jax
import jax.numpy as jnp
from jax import lax
from jax.experimental import pallas as pl
from jax.experimental.pallas import tpu as pltpu
from jax.sharding import PartitionSpec as P

HD = 128
FACTOR = 1.0 / math.sqrt(HD)
LOG2_FACTOR = FACTOR * math.log2(math.e)
MESH = pl.DeviceIdType.MESH
STRIDE = 13
OWNERS = 4


def contract(left, right):
    return lax.dot_general(
        left, right, (((1,), (1,)), ((), ())), preferred_element_type=jnp.float32
    )


def product(left, right):
    return jnp.dot(left, right, preferred_element_type=jnp.float32)


def attend(query, query_dot, key, key_dot, value, value_dot):
    scores = contract(query, key)
    scores_dot = contract(
        jnp.concatenate([query_dot, query], axis=1), jnp.concatenate([key, key_dot], axis=1)
    )
    top = jnp.max(scores, axis=1, keepdims=True)
    weights = jnp.exp2((scores - top) * LOG2_FACTOR)
    total = jnp.sum(weights, axis=1, keepdims=True)
    center = jnp.sum(weights * scores_dot, axis=1, keepdims=True) / total
    weights_dot = (weights * (scores_dot - center)).astype(jnp.bfloat16)
    both = product(weights.astype(jnp.bfloat16), jnp.concatenate([value, value_dot], axis=1))
    return top, total, center, both[:, :HD], both[:, HD:], product(weights_dot, value)


def join(one, two):
    top = jnp.maximum(one[0], two[0])
    parts = [(jnp.exp2((part[0] - top) * LOG2_FACTOR), *part[1:]) for part in (one, two)]
    total = sum(share * part for share, part, *_ in parts)
    center = sum(share * part * mean for share, part, mean, *_ in parts) / total
    output = sum(share * out for share, _, _, out, _, _ in parts)
    output_dot = sum(share * dot for share, _, _, _, dot, _ in parts)
    spread = sum(
        share * (dot + (mean - center) * out) for share, _, mean, out, _, dot in parts
    )
    return top, total, center, output, output_dot, spread


def finish(part):
    _, total, _, output, output_dot, spread = part
    inverse = 1.0 / total
    return (
        (output * inverse).astype(jnp.bfloat16),
        ((spread * FACTOR + output_dot) * inverse).astype(jnp.bfloat16),
    )


def kernel(groups, devices, *refs):
    ins, outs, refs = refs[:6], refs[6:8], refs[8:]
    kv_bufs, q_bufs, o_bufs, refs = refs[:4], refs[4:6], refs[6:8], refs[8:]
    stats, sums, kv_send, kv_recv, halo_send, halo_recv, q_send, q_recv, o_send, o_recv = refs
    query, key_in, value, query_dot, key_dot, value_dot = ins
    kvs = (key_in, key_dot, value, value_dot)
    qs = (query, query_dot)
    group, me = lax.axis_index("tm"), lax.axis_index("head")
    tokens = query.shape[1]
    half = tokens // 2
    width = tokens * devices
    rows = OWNERS * tokens
    high, odd = group // 2, lax.rem(group, 2)
    next_place = (lax.rem(group + 1, groups), me ^ (odd * 4))
    prior_place = (lax.rem(group + groups - 1, groups), me ^ ((1 - odd) * 4))

    def head_columns(device):
        return pl.ds(pl.multiple_of((device ^ (high * 4)) * HD, HD), HD)

    def rows_of(place, size):
        return pl.ds(pl.multiple_of(place * size, size), size)

    def partner(step):
        offset = lax.rem(step * STRIDE, devices)
        x = lax.rem(me // 8 + offset // 8, 4)
        y = lax.rem(me // 4 + offset // 4, 2)
        z = lax.rem(me + offset, 4)
        return x * 8 + y * 4 + z

    def send_all(source, dest, send, recv):
        def step(index, carry):
            peer = partner(index)
            pltpu.make_async_remote_copy(
                source(peer), dest, send, recv, device_id=(group, peer), device_id_type=MESH
            ).start()
            return carry

        lax.fori_loop(1, devices, step, 0)
        pltpu.make_async_copy(source(me), dest, recv).start()

    def send_keys(frame, part):
        for i, (source, buf) in enumerate(zip(kvs, kv_bufs)):
            send_all(
                lambda peer: source.at[frame, pl.ds(part * half, half), head_columns(peer)],
                buf.at[frame + 1, part, rows_of(me, half)],
                kv_send.at[frame, part, i],
                kv_recv.at[frame, part, i],
            )

    def send_queries(frame):
        for i, (source, buf) in enumerate(zip(qs, q_bufs)):
            send_all(
                lambda peer: source.at[frame, :, head_columns(peer)],
                buf.at[frame, rows_of(me, tokens)],
                q_send.at[frame, i],
                q_recv.at[frame, i],
            )

    def await_bytes(ref, semaphore):
        pltpu.make_async_copy(ref, ref, semaphore).wait()

    def await_keys(frame, part):
        for i, buf in enumerate(kv_bufs):
            await_bytes(buf.at[frame + 1, part], kv_recv.at[frame, part, i])

    def await_queries(frame):
        for i, buf in enumerate(q_bufs):
            await_bytes(buf.at[frame], q_recv.at[frame, i])

    def halo(i, buf):
        return pltpu.make_async_remote_copy(
            buf.at[2], buf.at[0], halo_send.at[i], halo_recv.at[i],
            device_id=next_place, device_id_type=MESH,
        )

    def block_of(index):
        x = lax.rem(me // 8 + (index + 1) // 2, 4)
        y = lax.rem(me // 4 + index + 1, 2)
        return x * 2 + y

    def load_queries(frame, block):
        return [buf[frame, rows_of(block, rows)] for buf in q_bufs]

    def load_keys(slot, part=None):
        if part is not None:
            return [buf[slot, part] for buf in kv_bufs]
        return [buf[slot].reshape(width, HD) for buf in kv_bufs]

    def load_state(block):
        place = rows_of(block, rows)
        return [stats[i, place] for i in range(3)] + [sums[i, place] for i in range(3)]

    def store_state(block, state):
        place = rows_of(block, rows)
        for i in range(3):
            stats[i, place] = state[i]
            sums[i, place] = state[i + 3]

    def send_outputs(frame, block, results):
        for buf, result in zip(o_bufs, results):
            buf[frame, rows_of(block, rows)] = result
        for j in range(OWNERS):
            owner = block * OWNERS + lax.rem(me + j, OWNERS)
            for i, (buf, target) in enumerate(zip(o_bufs, outs)):
                source = buf.at[frame, rows_of(owner, tokens)]
                dest = target.at[frame, :, head_columns(me)]

                def push():
                    pltpu.make_async_remote_copy(
                        source, dest, o_send.at[i], o_recv.at[i],
                        device_id=(group, owner), device_id_type=MESH,
                    ).start()

                if j:
                    push()
                else:
                    own = owner == me
                    pl.when(jnp.logical_not(own))(push)

                    @pl.when(own)
                    def _():
                        pltpu.make_async_copy(source, dest, o_recv.at[i]).start()

    def each_block(body):
        def step(index, carry):
            body(block_of(index))
            return carry

        lax.fori_loop(0, width // rows, step, 0)

    barrier = pltpu.get_barrier_semaphore()

    def greet(step, carry):
        peer = lax.rem(me + step, devices)
        pl.semaphore_signal(barrier, inc=1, device_id=(group, peer), device_id_type=MESH)
        return carry

    lax.fori_loop(1, devices, greet, 0)
    for place in (prior_place, next_place):
        pl.semaphore_signal(barrier, inc=1, device_id=place, device_id_type=MESH)
    pl.semaphore_wait(barrier, devices + 1)

    send_keys(1, 0)
    send_keys(1, 1)
    send_queries(1)
    await_keys(1, 0)
    await_keys(1, 1)
    for i, buf in enumerate(kv_bufs):
        halo(i, buf).start()
    send_keys(0, 0)
    send_keys(0, 1)
    send_queries(0)

    await_queries(1)

    @each_block
    def _(block):
        store_state(block, attend(*load_queries(1, block), *load_keys(2)))

    await_keys(0, 0)

    @each_block
    def _(block):
        part = attend(*load_queries(1, block), *load_keys(1, 0))
        store_state(block, join(load_state(block), part))

    await_keys(0, 1)

    @each_block
    def _(block):
        part = attend(*load_queries(1, block), *load_keys(1, 1))
        send_outputs(1, block, finish(join(load_state(block), part)))

    await_queries(0)
    for i, buf in enumerate(kv_bufs):
        await_bytes(buf.at[0], halo_recv.at[i])

    @each_block
    def _(block):
        queries = load_queries(0, block)
        own = attend(*queries, *load_keys(1))
        prior = attend(*queries, *load_keys(0))
        first = group == 0
        prior = (jnp.where(first, -1e30, prior[0]), jnp.where(first, 0.0, prior[1]), *prior[2:])
        send_outputs(0, block, finish(join(prior, own)))

    for i, buf in enumerate(kv_bufs):
        await_bytes(buf.at[2], halo_send.at[i])
        for frame in (0, 1):
            for part in (0, 1):
                sent = buf.at[frame + 1, part, pl.ds(0, (devices - 1) * half)]
                await_bytes(sent, kv_send.at[frame, part, i])
    for i in (0, 1):
        for frame in (0, 1):
            sent = q_bufs[i].at[frame, pl.ds(0, (devices - 1) * tokens)]
            await_bytes(sent, q_send.at[frame, i])
        await_bytes(o_bufs[i].at[:, pl.ds(0, (devices - 1) * tokens)], o_send.at[i])
        await_bytes(outs[i], o_recv.at[i])


def per_device(*args):
    groups, devices = lax.axis_size("tm"), lax.axis_size("head")
    frames, tokens, model = args[0].shape
    width = tokens * devices
    bf16 = jnp.bfloat16
    kv = pltpu.VMEM((frames + 1, 2, width // 2, HD), bf16)
    q = pltpu.VMEM((frames, width, HD), bf16)
    stats = pltpu.VMEM((3, width, 1), jnp.float32)
    sums = pltpu.VMEM((3, width, HD), jnp.float32)
    dma = pltpu.SemaphoreType.DMA
    sems = [dma(dims) for dims in ((2, 2, 4), (2, 2, 4), (4,), (4,), (2, 2), (2, 2), (2,), (2,))]
    return pl.pallas_call(
        functools.partial(kernel, groups, devices),
        out_shape=[jax.ShapeDtypeStruct((frames, tokens, model), bf16)] * 2,
        in_specs=[pl.BlockSpec(memory_space=pl.ANY)] * 6,
        out_specs=[pl.BlockSpec(memory_space=pl.ANY)] * 2,
        scratch_shapes=[kv] * 4 + [q] * 4 + [stats, sums] + sems,
        compiler_params=pltpu.CompilerParams(
            collective_id=0, has_side_effects=True, vmem_limit_bytes=56 * 1024 * 1024
        ),
    )(*args)


def solution(mesh):
    spec = P("tm", "head", None)
    return jax.shard_map(
        per_device, mesh=mesh, in_specs=(spec,) * 6, out_specs=(spec, spec), check_vma=False
    )
```

```python
import functools
import math

import jax
import jax.numpy as jnp
from jax import lax
from jax.experimental import pallas as pl
from jax.experimental.pallas import tpu as pltpu
from jax.sharding import PartitionSpec as P

HD = 128
FACTOR = 1.0 / math.sqrt(HD)
LOG2_FACTOR = FACTOR * math.log2(math.e)
MESH = pl.DeviceIdType.MESH
STRIDE = 13
OWNERS = 8


def contract(left, right):
    return lax.dot_general(
        left, right, (((1,), (1,)), ((), ())), preferred_element_type=jnp.float32
    )


def product(left, right):
    return jnp.dot(left, right, preferred_element_type=jnp.float32)


def attend(query, query_dot, key, key_dot, value, value_dot):
    scores = contract(query, key)
    scores_dot = contract(
        jnp.concatenate([query_dot, query], axis=1), jnp.concatenate([key, key_dot], axis=1)
    )
    top = jnp.max(scores, axis=1, keepdims=True)
    weights = jnp.exp2((scores - top) * LOG2_FACTOR)
    total = jnp.sum(weights, axis=1, keepdims=True)
    center = jnp.sum(weights * scores_dot, axis=1, keepdims=True) / total
    weights_dot = (weights * (scores_dot - center)).astype(jnp.bfloat16)
    both = product(weights.astype(jnp.bfloat16), jnp.concatenate([value, value_dot], axis=1))
    return top, total, center, both[:, :HD], both[:, HD:], product(weights_dot, value)


def join(one, two):
    top = jnp.maximum(one[0], two[0])
    parts = [(jnp.exp2((part[0] - top) * LOG2_FACTOR), *part[1:]) for part in (one, two)]
    total = sum(share * part for share, part, *_ in parts)
    center = sum(share * part * mean for share, part, mean, *_ in parts) / total
    output = sum(share * out for share, _, _, out, _, _ in parts)
    output_dot = sum(share * dot for share, _, _, _, dot, _ in parts)
    spread = sum(
        share * (dot + (mean - center) * out) for share, _, mean, out, _, dot in parts
    )
    return top, total, center, output, output_dot, spread


def finish(part):
    _, total, _, output, output_dot, spread = part
    inverse = 1.0 / total
    return (
        (output * inverse).astype(jnp.bfloat16),
        ((spread * FACTOR + output_dot) * inverse).astype(jnp.bfloat16),
    )


def kernel(groups, devices, *refs):
    ins, outs, refs = refs[:6], refs[6:8], refs[8:]
    kv_bufs, q_bufs, o_bufs, refs = refs[:4], refs[4:6], refs[6:8], refs[8:]
    stats, sums, kv_send, kv_recv, halo_send, halo_recv, q_send, q_recv, o_send, o_recv = refs
    query, key_in, value, query_dot, key_dot, value_dot = ins
    kvs = (key_in, key_dot, value, value_dot)
    qs = (query, query_dot)
    group, me = lax.axis_index("tm"), lax.axis_index("head")
    tokens = query.shape[1]
    half = tokens // 2
    width = tokens * devices
    rows = OWNERS * tokens
    high, odd = group // 2, lax.rem(group, 2)
    next_place = (lax.rem(group + 1, groups), me ^ (odd * 4))
    prior_place = (lax.rem(group + groups - 1, groups), me ^ ((1 - odd) * 4))

    def head_columns(device):
        return pl.ds(pl.multiple_of((device ^ (high * 4)) * HD, HD), HD)

    def rows_of(place, size):
        return pl.ds(pl.multiple_of(place * size, size), size)

    def partner(step):
        offset = lax.rem(step * STRIDE, devices)
        x = lax.rem(me // 8 + offset // 8, 4)
        y = lax.rem(me // 4 + offset // 4, 2)
        z = lax.rem(me + offset, 4)
        return x * 8 + y * 4 + z

    def send_all(source, dest, send, recv):
        def step(index, carry):
            peer = partner(index)
            pltpu.make_async_remote_copy(
                source(peer), dest, send, recv, device_id=(group, peer), device_id_type=MESH
            ).start()
            return carry

        lax.fori_loop(1, devices, step, 0)
        pltpu.make_async_copy(source(me), dest, recv).start()

    def send_keys(frame, part):
        for i, (source, buf) in enumerate(zip(kvs, kv_bufs)):
            send_all(
                lambda peer: source.at[frame, pl.ds(part * half, half), head_columns(peer)],
                buf.at[frame + 1, part, rows_of(me, half)],
                kv_send.at[frame, part, i],
                kv_recv.at[frame, part, i],
            )

    def send_queries(frame):
        for i, (source, buf) in enumerate(zip(qs, q_bufs)):
            send_all(
                lambda peer: source.at[frame, :, head_columns(peer)],
                buf.at[frame, rows_of(me, tokens)],
                q_send.at[frame, i],
                q_recv.at[frame, i],
            )

    def await_bytes(ref, semaphore):
        pltpu.make_async_copy(ref, ref, semaphore).wait()

    def await_keys(frame, part):
        for i, buf in enumerate(kv_bufs):
            await_bytes(buf.at[frame + 1, part], kv_recv.at[frame, part, i])

    def await_queries(frame):
        for i, buf in enumerate(q_bufs):
            await_bytes(buf.at[frame], q_recv.at[frame, i])

    def halo(i, buf):
        return pltpu.make_async_remote_copy(
            buf.at[2], buf.at[0], halo_send.at[i], halo_recv.at[i],
            device_id=next_place, device_id_type=MESH,
        )

    def block_of(index):
        return lax.rem(me // OWNERS + index + 1, devices // OWNERS)

    def load_queries(frame, block):
        return [buf[frame, rows_of(block, rows)] for buf in q_bufs]

    def load_keys(slot, part=None):
        if part is not None:
            return [buf[slot, part] for buf in kv_bufs]
        return [buf[slot].reshape(width, HD) for buf in kv_bufs]

    def load_state(frame, block):
        place = rows_of(block, rows)
        return [stats[frame, i, place] for i in range(3)] + [sums[frame, i, place] for i in range(3)]

    def store_state(frame, block, state):
        place = rows_of(block, rows)
        for i in range(3):
            stats[frame, i, place] = state[i]
            sums[frame, i, place] = state[i + 3]

    def send_outputs(frame, block, results):
        for buf, result in zip(o_bufs, results):
            buf[frame, rows_of(block, rows)] = result
        for j in range(OWNERS):
            owner = block * OWNERS + lax.rem(me + j, OWNERS)
            for i, (buf, target) in enumerate(zip(o_bufs, outs)):
                source = buf.at[frame, rows_of(owner, tokens)]
                dest = target.at[frame, :, head_columns(me)]

                def push():
                    pltpu.make_async_remote_copy(
                        source, dest, o_send.at[i], o_recv.at[i],
                        device_id=(group, owner), device_id_type=MESH,
                    ).start()

                if j:
                    push()
                else:
                    own = owner == me
                    pl.when(jnp.logical_not(own))(push)

                    @pl.when(own)
                    def _():
                        pltpu.make_async_copy(source, dest, o_recv.at[i]).start()

    def each_block(body):
        def step(index, carry):
            body(block_of(index))
            return carry

        lax.fori_loop(0, width // rows, step, 0)

    barrier = pltpu.get_barrier_semaphore()

    def greet(step, carry):
        peer = lax.rem(me + step, devices)
        pl.semaphore_signal(barrier, inc=1, device_id=(group, peer), device_id_type=MESH)
        return carry

    lax.fori_loop(1, devices, greet, 0)
    for place in (prior_place, next_place):
        pl.semaphore_signal(barrier, inc=1, device_id=place, device_id_type=MESH)
    pl.semaphore_wait(barrier, devices + 1)

    send_keys(1, 0)
    send_keys(1, 1)
    send_queries(1)
    await_keys(1, 0)
    await_keys(1, 1)
    for i, buf in enumerate(kv_bufs):
        halo(i, buf).start()
    send_keys(0, 0)
    send_queries(0)
    send_keys(0, 1)
    await_queries(1)

    @each_block
    def _(block):
        store_state(1, block, attend(*load_queries(1, block), *load_keys(2)))

    await_keys(0, 0)

    @each_block
    def _(block):
        part = attend(*load_queries(1, block), *load_keys(1, 0))
        store_state(1, block, join(load_state(1, block), part))

    await_queries(0)
    for i, buf in enumerate(kv_bufs):
        await_bytes(buf.at[0], halo_recv.at[i])

    @each_block
    def _(block):
        top, total, *rest = attend(*load_queries(0, block), *load_keys(0))
        first = group == 0
        top, total = jnp.where(first, -1e30, top), jnp.where(first, 0.0, total)
        store_state(0, block, (top, total, *rest))

    await_keys(0, 1)

    @each_block
    def _(block):
        part = attend(*load_queries(1, block), *load_keys(1, 1))
        send_outputs(1, block, finish(join(load_state(1, block), part)))

    @each_block
    def _(block):
        part = attend(*load_queries(0, block), *load_keys(1))
        send_outputs(0, block, finish(join(load_state(0, block), part)))

    for i, buf in enumerate(kv_bufs):
        await_bytes(buf.at[2], halo_send.at[i])
        for frame in (0, 1):
            for part in (0, 1):
                sent = buf.at[frame + 1, part, pl.ds(0, (devices - 1) * half)]
                await_bytes(sent, kv_send.at[frame, part, i])
    for i in (0, 1):
        for frame in (0, 1):
            sent = q_bufs[i].at[frame, pl.ds(0, (devices - 1) * tokens)]
            await_bytes(sent, q_send.at[frame, i])
        await_bytes(o_bufs[i].at[:, pl.ds(0, (devices - 1) * tokens)], o_send.at[i])
        await_bytes(outs[i], o_recv.at[i])


def per_device(*args):
    groups, devices = lax.axis_size("tm"), lax.axis_size("head")
    frames, tokens, model = args[0].shape
    width = tokens * devices
    bf16 = jnp.bfloat16
    kv = pltpu.VMEM((frames + 1, 2, width // 2, HD), bf16)
    q = pltpu.VMEM((frames, width, HD), bf16)
    stats = pltpu.VMEM((frames, 3, width, 1), jnp.float32)
    sums = pltpu.VMEM((frames, 3, width, HD), jnp.float32)
    dma = pltpu.SemaphoreType.DMA
    sems = [dma(dims) for dims in ((2, 2, 4), (2, 2, 4), (4,), (4,), (2, 2), (2, 2), (2,), (2,))]
    return pl.pallas_call(
        functools.partial(kernel, groups, devices),
        out_shape=[pltpu.VMEM((frames, tokens, model), bf16)] * 2,
        in_specs=[pl.BlockSpec(memory_space=pl.ANY)] * 6,
        out_specs=[pl.BlockSpec(memory_space=pltpu.VMEM)] * 2,
        scratch_shapes=[kv] * 4 + [q] * 4 + [stats, sums] + sems,
        compiler_params=pltpu.CompilerParams(
            collective_id=0, has_side_effects=True, vmem_limit_bytes=56 * 1024 * 1024
        ),
    )(*args)


def solution(mesh):
    spec = P("tm", "head", None)
    return jax.shard_map(
        per_device, mesh=mesh, in_specs=(spec,) * 6, out_specs=(spec, spec), check_vma=False
    )
```

```python
import functools
import math

import jax
import jax.numpy as jnp
from jax import lax
from jax.experimental import pallas as pl
from jax.experimental.pallas import tpu as pltpu
from jax.sharding import PartitionSpec as P

HD = 128
FACTOR = 1.0 / math.sqrt(HD)
LOG2_FACTOR = FACTOR * math.log2(math.e)
MESH = pl.DeviceIdType.MESH
STRIDE = 13
OWNERS = 8


def contract(left, right):
    return lax.dot_general(
        left, right, (((1,), (1,)), ((), ())), preferred_element_type=jnp.float32
    )


def product(left, right):
    return jnp.dot(left, right, preferred_element_type=jnp.float32)


def attend(query, query_dot, key, key_dot, value, value_dot):
    scores = contract(query, key)
    scores_dot = contract(
        jnp.concatenate([query_dot, query], axis=1), jnp.concatenate([key, key_dot], axis=1)
    )
    top = jnp.max(scores, axis=1, keepdims=True)
    weights = jnp.exp2((scores - top) * LOG2_FACTOR)
    total = jnp.sum(weights, axis=1, keepdims=True)
    center = jnp.sum(weights * scores_dot, axis=1, keepdims=True) / total
    weights_dot = (weights * (scores_dot - center)).astype(jnp.bfloat16)
    both = product(weights.astype(jnp.bfloat16), jnp.concatenate([value, value_dot], axis=1))
    return top, total, center, both[:, :HD], both[:, HD:], product(weights_dot, value)


def join(one, two):
    top = jnp.maximum(one[0], two[0])
    parts = [(jnp.exp2((part[0] - top) * LOG2_FACTOR), *part[1:]) for part in (one, two)]
    total = sum(share * part for share, part, *_ in parts)
    center = sum(share * part * mean for share, part, mean, *_ in parts) / total
    output = sum(share * out for share, _, _, out, _, _ in parts)
    output_dot = sum(share * dot for share, _, _, _, dot, _ in parts)
    spread = sum(
        share * (dot + (mean - center) * out) for share, _, mean, out, _, dot in parts
    )
    return top, total, center, output, output_dot, spread


def finish(part):
    _, total, _, output, output_dot, spread = part
    inverse = 1.0 / total
    return (
        (output * inverse).astype(jnp.bfloat16),
        ((spread * FACTOR + output_dot) * inverse).astype(jnp.bfloat16),
    )


def kernel(groups, devices, *refs):
    ins, outs, refs = refs[:6], refs[6:8], refs[8:]
    kv_bufs, q_bufs, o_bufs, refs = refs[:4], refs[4:6], refs[6:8], refs[8:]
    stats, sums, kv_send, kv_recv, halo_send, halo_recv, q_send, q_recv, o_send, o_recv = refs
    query, key_in, value, query_dot, key_dot, value_dot = ins
    kvs = (key_in, key_dot, value, value_dot)
    qs = (query, query_dot)
    group, me = lax.axis_index("tm"), lax.axis_index("head")
    tokens = query.shape[1]
    half = tokens // 2
    width = tokens * devices
    rows = OWNERS * tokens
    high, odd = group // 2, lax.rem(group, 2)
    next_place = (lax.rem(group + 1, groups), me ^ (odd * 4))
    prior_place = (lax.rem(group + groups - 1, groups), me ^ ((1 - odd) * 4))

    def head_columns(device):
        return pl.ds(pl.multiple_of((device ^ (high * 4)) * HD, HD), HD)

    def rows_of(place, size):
        return pl.ds(pl.multiple_of(place * size, size), size)

    def partner(step):
        offset = lax.rem(step * STRIDE, devices)
        x = lax.rem(me // 8 + offset // 8, 4)
        y = lax.rem(me // 4 + offset // 4, 2)
        z = lax.rem(me + offset, 4)
        return x * 8 + y * 4 + z

    def send_all(source, dest, send, recv):
        def step(index, carry):
            peer = partner(index)
            pltpu.make_async_remote_copy(
                source(peer), dest, send, recv, device_id=(group, peer), device_id_type=MESH
            ).start()
            return carry

        lax.fori_loop(1, devices, step, 0)
        pltpu.make_async_copy(source(me), dest, recv).start()

    def send_keys(frame, part, size):
        for i, (source, buf) in enumerate(zip(kvs, kv_bufs)):
            send_all(
                lambda peer: source.at[frame, pl.ds(part * size, size), head_columns(peer)],
                buf.at[frame + 1, rows_of(part * devices + me, size)],
                kv_send.at[frame, part, i],
                kv_recv.at[frame, part, i],
            )

    def send_queries(frame):
        for i, (source, buf) in enumerate(zip(qs, q_bufs)):
            send_all(
                lambda peer: source.at[frame, :, head_columns(peer)],
                buf.at[frame, rows_of(my_block * OWNERS + my_slot, tokens)],
                q_send.at[frame, i],
                q_recv.at[frame, i],
            )

    def await_bytes(ref, semaphore):
        pltpu.make_async_copy(ref, ref, semaphore).wait()

    def await_keys(frame, part, size):
        for i, buf in enumerate(kv_bufs):
            await_bytes(buf.at[frame + 1, pl.ds(0, devices * size)], kv_recv.at[frame, part, i])

    def await_queries(frame):
        for i, buf in enumerate(q_bufs):
            await_bytes(buf.at[frame], q_recv.at[frame, i])

    def halo(i, buf):
        return pltpu.make_async_remote_copy(
            buf.at[2], buf.at[0], halo_send.at[i], halo_recv.at[i],
            device_id=next_place, device_id_type=MESH,
        )

    my_x, my_y, my_z = me // 8, lax.rem(me // 4, 2), lax.rem(me, 4)
    my_block = lax.rem(my_x + my_z, 4)
    my_slot = my_x * 2 + my_y

    def block_of(index):
        return lax.rem(my_block + index + 1, 4)

    def load_queries(frame, block):
        return [buf[frame, rows_of(block, rows)] for buf in q_bufs]

    def load_keys(slot, part=None):
        if part is not None:
            return [buf[slot, pl.ds(part * (width // 2), width // 2)] for buf in kv_bufs]
        return [buf[slot] for buf in kv_bufs]

    def load_state(frame, block):
        place = rows_of(block, rows)
        return [stats[frame, i, place] for i in range(3)] + [sums[frame, i, place] for i in range(3)]

    def store_state(frame, block, state):
        place = rows_of(block, rows)
        for i in range(3):
            stats[frame, i, place] = state[i]
            sums[frame, i, place] = state[i + 3]

    def send_outputs(frame, block, results):
        for buf, result in zip(o_bufs, results):
            buf[frame, rows_of(block, rows)] = result
        for j in range(OWNERS):
            slot = lax.rem(my_slot + j, OWNERS)
            x, y = slot // 2, lax.rem(slot, 2)
            owner = x * 8 + y * 4 + lax.rem(block + 4 - x, 4)
            for i, (buf, target) in enumerate(zip(o_bufs, outs)):
                source = buf.at[frame, rows_of(block * OWNERS + slot, tokens)]
                dest = target.at[frame, :, head_columns(me)]

                def push():
                    pltpu.make_async_remote_copy(
                        source, dest, o_send.at[i], o_recv.at[i],
                        device_id=(group, owner), device_id_type=MESH,
                    ).start()

                if j:
                    push()
                else:
                    own = owner == me
                    pl.when(jnp.logical_not(own))(push)

                    @pl.when(own)
                    def _():
                        pltpu.make_async_copy(source, dest, o_recv.at[i]).start()

    def each_block(body):
        def step(index, carry):
            body(block_of(index))
            return carry

        lax.fori_loop(0, width // rows, step, 0)

    barrier = pltpu.get_barrier_semaphore()

    def greet(step, carry):
        peer = lax.rem(me + step, devices)
        pl.semaphore_signal(barrier, inc=1, device_id=(group, peer), device_id_type=MESH)
        return carry

    lax.fori_loop(1, devices, greet, 0)
    for place in (prior_place, next_place):
        pl.semaphore_signal(barrier, inc=1, device_id=place, device_id_type=MESH)
    pl.semaphore_wait(barrier, devices + 1)

    send_keys(1, 0, tokens)
    send_queries(1)
    await_keys(1, 0, tokens)
    for i, buf in enumerate(kv_bufs):
        halo(i, buf).start()
    send_keys(0, 0, half)
    send_queries(0)
    send_keys(0, 1, half)
    await_queries(1)

    @each_block
    def _(block):
        store_state(1, block, attend(*load_queries(1, block), *load_keys(2)))

    await_keys(0, 0, half)

    @each_block
    def _(block):
        part = attend(*load_queries(1, block), *load_keys(1, 0))
        store_state(1, block, join(load_state(1, block), part))

    await_queries(0)
    for i, buf in enumerate(kv_bufs):
        await_bytes(buf.at[0], halo_recv.at[i])

    @each_block
    def _(block):
        top, total, *rest = attend(*load_queries(0, block), *load_keys(0))
        first = group == 0
        top, total = jnp.where(first, -1e30, top), jnp.where(first, 0.0, total)
        store_state(0, block, (top, total, *rest))

    await_keys(0, 1, half)

    @each_block
    def _(block):
        part = attend(*load_queries(1, block), *load_keys(1, 1))
        send_outputs(1, block, finish(join(load_state(1, block), part)))

    @each_block
    def _(block):
        part = attend(*load_queries(0, block), *load_keys(1))
        send_outputs(0, block, finish(join(load_state(0, block), part)))

    for i, buf in enumerate(kv_bufs):
        await_bytes(buf.at[2], halo_send.at[i])
        for frame, part, size in ((1, 0, tokens), (0, 0, half), (0, 1, half)):
            sent = buf.at[frame + 1, pl.ds(0, (devices - 1) * size)]
            await_bytes(sent, kv_send.at[frame, part, i])
    for i in (0, 1):
        for frame in (0, 1):
            sent = q_bufs[i].at[frame, pl.ds(0, (devices - 1) * tokens)]
            await_bytes(sent, q_send.at[frame, i])
        await_bytes(o_bufs[i].at[:, pl.ds(0, (devices - 1) * tokens)], o_send.at[i])
        await_bytes(outs[i], o_recv.at[i])


def per_device(*args):
    groups, devices = lax.axis_size("tm"), lax.axis_size("head")
    frames, tokens, model = args[0].shape
    width = tokens * devices
    bf16 = jnp.bfloat16
    kv = pltpu.VMEM((frames + 1, width, HD), bf16)
    q = pltpu.VMEM((frames, width, HD), bf16)
    stats = pltpu.VMEM((frames, 3, width, 1), jnp.float32)
    sums = pltpu.VMEM((frames, 3, width, HD), jnp.float32)
    dma = pltpu.SemaphoreType.DMA
    sems = [dma(dims) for dims in ((2, 2, 4), (2, 2, 4), (4,), (4,), (2, 2), (2, 2), (2,), (2,))]
    return pl.pallas_call(
        functools.partial(kernel, groups, devices),
        out_shape=[pltpu.VMEM((frames, tokens, model), bf16)] * 2,
        in_specs=[pl.BlockSpec(memory_space=pl.ANY)] * 6,
        out_specs=[pl.BlockSpec(memory_space=pltpu.VMEM)] * 2,
        scratch_shapes=[kv] * 4 + [q] * 4 + [stats, sums] + sems,
        compiler_params=pltpu.CompilerParams(
            collective_id=0, has_side_effects=True, vmem_limit_bytes=56 * 1024 * 1024
        ),
    )(*args)


def solution(mesh):
    spec = P("tm", "head", None)
    return jax.shard_map(
        per_device, mesh=mesh, in_specs=(spec,) * 6, out_specs=(spec, spec), check_vma=False
    )
```

```python
import functools
import math

import jax
import jax.numpy as jnp
from jax import lax
from jax.experimental import pallas as pl
from jax.experimental.pallas import tpu as pltpu
from jax.sharding import PartitionSpec as P

HD = 128
FACTOR = 1.0 / math.sqrt(HD)
LOG2_FACTOR = FACTOR * math.log2(math.e)
MESH = pl.DeviceIdType.MESH
STRIDE = 13
OWNERS = 8


def contract(left, right):
    return lax.dot_general(
        left, right, (((1,), (1,)), ((), ())), preferred_element_type=jnp.float32
    )


def product(left, right):
    return jnp.dot(left, right, preferred_element_type=jnp.float32)


def attend(query, query_dot, key, key_dot, value, value_dot):
    scores = contract(query, key)
    scores_dot = contract(
        jnp.concatenate([query_dot, query], axis=1), jnp.concatenate([key, key_dot], axis=1)
    )
    top = jnp.max(scores, axis=1, keepdims=True)
    weights = jnp.exp2((scores - top) * LOG2_FACTOR)
    total = jnp.sum(weights, axis=1, keepdims=True)
    center = jnp.sum(weights * scores_dot, axis=1, keepdims=True) / total
    weights_dot = (weights * (scores_dot - center)).astype(jnp.bfloat16)
    both = product(weights.astype(jnp.bfloat16), jnp.concatenate([value, value_dot], axis=1))
    return top, total, center, both[:, :HD], both[:, HD:], product(weights_dot, value)


def join(one, two):
    top = jnp.maximum(one[0], two[0])
    parts = [(jnp.exp2((part[0] - top) * LOG2_FACTOR), *part[1:]) for part in (one, two)]
    total = sum(share * part for share, part, *_ in parts)
    center = sum(share * part * mean for share, part, mean, *_ in parts) / total
    output = sum(share * out for share, _, _, out, _, _ in parts)
    output_dot = sum(share * dot for share, _, _, _, dot, _ in parts)
    spread = sum(
        share * (dot + (mean - center) * out) for share, _, mean, out, _, dot in parts
    )
    return top, total, center, output, output_dot, spread


def finish(part):
    _, total, _, output, output_dot, spread = part
    inverse = 1.0 / total
    return (
        (output * inverse).astype(jnp.bfloat16),
        ((spread * FACTOR + output_dot) * inverse).astype(jnp.bfloat16),
    )


def kernel(groups, devices, *refs):
    ins, outs, refs = refs[:6], refs[6:8], refs[8:]
    kv_bufs, q_bufs, o_bufs, refs = refs[:4], refs[4:6], refs[6:8], refs[8:]
    stats, sums, kv_send, kv_recv, halo_send, halo_recv, q_send, q_recv, o_send, o_recv = refs
    query, key_in, value, query_dot, key_dot, value_dot = ins
    kvs = (key_in, key_dot, value, value_dot)
    qs = (query, query_dot)
    group, me = lax.axis_index("tm"), lax.axis_index("head")
    tokens = query.shape[1]
    half = tokens // 2
    width = tokens * devices
    rows = OWNERS * tokens
    high, odd = group // 2, lax.rem(group, 2)
    next_place = (lax.rem(group + 1, groups), me ^ (odd * 4))
    prior_place = (lax.rem(group + groups - 1, groups), me ^ ((1 - odd) * 4))

    def head_columns(device):
        return pl.ds(pl.multiple_of((device ^ (high * 4)) * HD, HD), HD)

    def rows_of(place, size):
        return pl.ds(pl.multiple_of(place * size, size), size)

    def partner(step):
        offset = lax.rem(step * STRIDE, devices)
        x = lax.rem(me // 8 + offset // 8, 4)
        y = lax.rem(me // 4 + offset // 4, 2)
        z = lax.rem(me + offset, 4)
        return x * 8 + y * 4 + z

    def send_all(source, dest, send, recv):
        def step(index, carry):
            peer = partner(index)
            pltpu.make_async_remote_copy(
                source(peer), dest, send, recv, device_id=(group, peer), device_id_type=MESH
            ).start()
            return carry

        lax.fori_loop(1, devices, step, 0)
        pltpu.make_async_copy(source(me), dest, recv).start()

    def send_keys(frame, part, size):
        for i, (source, buf) in enumerate(zip(kvs, kv_bufs)):
            send_all(
                lambda peer: source.at[frame, pl.ds(part * size, size), head_columns(peer)],
                buf.at[frame + 1, rows_of(part * devices + me, size)],
                kv_send.at[frame, part, i],
                kv_recv.at[frame, part, i],
            )

    def send_queries(frame):
        for i, (source, buf) in enumerate(zip(qs, q_bufs)):
            send_all(
                lambda peer: source.at[frame, :, head_columns(peer)],
                buf.at[frame, rows_of(my_block * OWNERS + my_slot, tokens)],
                q_send.at[frame, i],
                q_recv.at[frame, i],
            )

    def await_bytes(ref, semaphore):
        pltpu.make_async_copy(ref, ref, semaphore).wait()

    def await_keys(frame, part, size):
        for i, buf in enumerate(kv_bufs):
            await_bytes(buf.at[frame + 1, pl.ds(0, devices * size)], kv_recv.at[frame, part, i])

    def await_queries(frame):
        for i, buf in enumerate(q_bufs):
            await_bytes(buf.at[frame], q_recv.at[frame, i])

    def halo(i, buf):
        return pltpu.make_async_remote_copy(
            buf.at[2], buf.at[0], halo_send.at[i], halo_recv.at[i],
            device_id=next_place, device_id_type=MESH,
        )

    my_x, my_y, my_z = me // 8, lax.rem(me // 4, 2), lax.rem(me, 4)
    my_block = lax.rem(my_x + my_z, 4)
    my_slot = my_x * 2 + my_y

    def block_of(index):
        return lax.rem(my_block + index + 1, 4)

    def load_queries(frame, block):
        return [buf[frame, rows_of(block, rows)] for buf in q_bufs]

    def load_keys(slot, part=None):
        if part is not None:
            return [buf[slot, pl.ds(part * (width // 2), width // 2)] for buf in kv_bufs]
        return [buf[slot] for buf in kv_bufs]

    def load_state(frame, block):
        place = rows_of(block, rows)
        return [stats[frame, i, place] for i in range(3)] + [sums[frame, i, place] for i in range(3)]

    def store_state(frame, block, state):
        place = rows_of(block, rows)
        for i in range(3):
            stats[frame, i, place] = state[i]
            sums[frame, i, place] = state[i + 3]

    def send_outputs(frame, block, results):
        for buf, result in zip(o_bufs, results):
            buf[frame, rows_of(block, rows)] = result
        for j in range(OWNERS):
            slot = lax.rem(my_slot + j, OWNERS)
            x, y = slot // 2, lax.rem(slot, 2)
            owner = x * 8 + y * 4 + lax.rem(block + 4 - x, 4)
            for i, (buf, target) in enumerate(zip(o_bufs, outs)):
                source = buf.at[frame, rows_of(block * OWNERS + slot, tokens)]
                dest = target.at[frame, :, head_columns(me)]

                def push():
                    pltpu.make_async_remote_copy(
                        source, dest, o_send.at[i], o_recv.at[i],
                        device_id=(group, owner), device_id_type=MESH,
                    ).start()

                if j:
                    push()
                else:
                    own = owner == me
                    pl.when(jnp.logical_not(own))(push)

                    @pl.when(own)
                    def _():
                        pltpu.make_async_copy(source, dest, o_recv.at[i]).start()

    def each_block(body):
        def step(index, carry):
            body(block_of(index))
            return carry

        lax.fori_loop(0, width // rows, step, 0)

    barrier = pltpu.get_barrier_semaphore()

    def greet(step, carry):
        peer = lax.rem(me + step, devices)
        pl.semaphore_signal(barrier, inc=1, device_id=(group, peer), device_id_type=MESH)
        return carry

    lax.fori_loop(1, devices, greet, 0)
    for place in (prior_place, next_place):
        pl.semaphore_signal(barrier, inc=1, device_id=place, device_id_type=MESH)
    pl.semaphore_wait(barrier, devices + 1)

    send_keys(1, 0, tokens)
    send_queries(1)
    await_keys(1, 0, tokens)
    for i, buf in enumerate(kv_bufs):
        halo(i, buf).start()
    send_queries(0)
    send_keys(0, 0, half)
    send_keys(0, 1, half)
    await_queries(1)

    @each_block
    def _(block):
        store_state(1, block, attend(*load_queries(1, block), *load_keys(2)))

    await_queries(0)
    for i, buf in enumerate(kv_bufs):
        await_bytes(buf.at[0], halo_recv.at[i])

    @each_block
    def _(block):
        top, total, *rest = attend(*load_queries(0, block), *load_keys(0))
        first = group == 0
        top, total = jnp.where(first, -1e30, top), jnp.where(first, 0.0, total)
        store_state(0, block, (top, total, *rest))

    await_keys(0, 0, half)

    @each_block
    def _(block):
        part = attend(*load_queries(1, block), *load_keys(1, 0))
        store_state(1, block, join(load_state(1, block), part))

    await_keys(0, 1, half)

    @each_block
    def _(block):
        part = attend(*load_queries(1, block), *load_keys(1, 1))
        send_outputs(1, block, finish(join(load_state(1, block), part)))

    @each_block
    def _(block):
        part = attend(*load_queries(0, block), *load_keys(1))
        send_outputs(0, block, finish(join(load_state(0, block), part)))

    for i, buf in enumerate(kv_bufs):
        await_bytes(buf.at[2], halo_send.at[i])
        for frame, part, size in ((1, 0, tokens), (0, 0, half), (0, 1, half)):
            sent = buf.at[frame + 1, pl.ds(0, (devices - 1) * size)]
            await_bytes(sent, kv_send.at[frame, part, i])
    for i in (0, 1):
        for frame in (0, 1):
            sent = q_bufs[i].at[frame, pl.ds(0, (devices - 1) * tokens)]
            await_bytes(sent, q_send.at[frame, i])
        await_bytes(o_bufs[i].at[:, pl.ds(0, (devices - 1) * tokens)], o_send.at[i])
        await_bytes(outs[i], o_recv.at[i])


def per_device(*args):
    groups, devices = lax.axis_size("tm"), lax.axis_size("head")
    frames, tokens, model = args[0].shape
    width = tokens * devices
    bf16 = jnp.bfloat16
    kv = pltpu.VMEM((frames + 1, width, HD), bf16)
    q = pltpu.VMEM((frames, width, HD), bf16)
    stats = pltpu.VMEM((frames, 3, width, 1), jnp.float32)
    sums = pltpu.VMEM((frames, 3, width, HD), jnp.float32)
    dma = pltpu.SemaphoreType.DMA
    sems = [dma(dims) for dims in ((2, 2, 4), (2, 2, 4), (4,), (4,), (2, 2), (2, 2), (2,), (2,))]
    return pl.pallas_call(
        functools.partial(kernel, groups, devices),
        out_shape=[pltpu.VMEM((frames, tokens, model), bf16)] * 2,
        in_specs=[pl.BlockSpec(memory_space=pl.ANY)] * 6,
        out_specs=[pl.BlockSpec(memory_space=pltpu.VMEM)] * 2,
        scratch_shapes=[kv] * 4 + [q] * 4 + [stats, sums] + sems,
        compiler_params=pltpu.CompilerParams(
            collective_id=0, has_side_effects=True, vmem_limit_bytes=56 * 1024 * 1024
        ),
    )(*args)


def solution(mesh):
    spec = P("tm", "head", None)
    return jax.shard_map(
        per_device, mesh=mesh, in_specs=(spec,) * 6, out_specs=(spec, spec), check_vma=False
    )
```
